512 devices in a mesh: tm: 128 (over x_lo, y, z), lat: 4 (over x_hi, core).
Axes of the slice: x: 4 (x_hi: 2, x_lo: 2; x = x_hi * 2 + x_lo), y: 4, z: 16, core: 2. Of those that a mesh axis runs over, the one named last changes fastest.
Arguments:
- trajectory: bfloat16 [512, 8, 64, 256], P('tm', 'lat'), may hold values from -6 to 6
- cotangent: bfloat16 [512, 8, 64, 256], P('tm', 'lat'), may hold values from -6 to 6
- conv_weight: bfloat16 [9, 256, 256], replicated, may hold values from -0.125 to 0.125
- proj_weight: bfloat16 [256, 256], replicated, may hold values from -0.375 to 0.375
- mixing: float32 [25, 256], replicated, may hold values from -2.5 to 2.5
- offsets: int32 [512], replicated, may hold values from 0 to 4
Outputs:
- grads: bfloat16 [512, 8, 64, 256], P('tm', 'lat')
The draws below stay inside these ranges and needn't reach their ends.
All inputs are finite; a program needn't handle non-finite values.
Results may differ from the reference program's by a relative error of at most 0.005.
Values may be sent and summed in bfloat16 or wider, within the bound.
No kernel may reach another device: no remote copies, remote signals or barrier semaphores. Data moves between devices by JAX's collectives and lax.ppermute only.
A program may use at most 64 MiB of HBM per device.

```python
import jax
import jax.numpy as jnp
from jax import lax

C = 256
LON = 64
FRAMES = 512
LATS = 8


def set_ends(drawn, own_key, least, top_value):
    longest = drawn.shape.index(max(drawn.shape))
    spots = []
    for shift in (0, 1):
        where = [jax.random.randint(jax.random.fold_in(own_key, axis), (), 0, length) for axis, length in enumerate(drawn.shape)]
        where[longest] = (where[longest] + shift) % drawn.shape[longest]
        spots.append(tuple(where))
    return drawn.at[spots[0]].set(least).at[spots[1]].set(top_value)


def level_of(rng, extent, cuts, least, largest):
    def one(position, parts):
        draws = jax.random.uniform(jax.random.fold_in(jax.random.fold_in(rng, 6), position), (parts,), jnp.float32, least / len(cuts), largest / len(cuts))
        return jnp.repeat(jnp.exp(draws), extent[position] // parts).reshape((-1,) + (1,) * (len(extent) - position - 1))

    gain = one(*cuts[0])
    for cut in cuts[1:]:
        gain = gain * one(*cut)
    return gain


def scatter_about(key, extent, spread, limit, pieces=(), kind=jnp.bfloat16):
    values = spread * jax.random.normal(key, extent, jnp.float32)
    if pieces:
        values = values * level_of(key, extent, pieces, -0.22, 0.18)
    return jnp.clip(values, -limit, limit).astype(kind)


def setup_inputs(seed: int = 0) -> dict:
    key_of = jax.random.split(jax.random.key(seed), 7)
    trajectory = scatter_about(key_of[0], (FRAMES, LATS, LON, C), 1.0, 6.0, ((0, 128), (1, 4)))
    cotangent = scatter_about(key_of[1], (FRAMES, LATS, LON, C), 1.0, 6.0, ((0, 128), (1, 4)))
    conv_weight = scatter_about(key_of[2], (9, C, C), (9 * C) ** -0.5, 0.125)
    proj_weight = scatter_about(key_of[3], (C, C), C ** -0.5, 0.375)
    mixing = scatter_about(key_of[4], (25, C), 5 ** -0.5, 2.5, (), jnp.float32)
    offsets = set_ends(jax.random.randint(key_of[5], (FRAMES,), 0, 5), jax.random.fold_in(key_of[5], 1), 0, 4).astype(jnp.int32)
    return dict(trajectory=trajectory, cotangent=cotangent, conv_weight=conv_weight, proj_weight=proj_weight, mixing=mixing, offsets=offsets)


def silu_slope(values):
    sigma = jax.nn.sigmoid(values)
    return sigma * (1.0 + values * (1.0 - sigma))

def conv_frame(frame, kernel):
    row_count, lon_count, channels = frame.shape
    padded = jnp.pad(frame, ((1, 1), (0, 0), (0, 0)))
    summed = jnp.zeros((row_count * lon_count, kernel.shape[2]), jnp.float32)
    for tap_index in range(9):
        lat_step = tap_index // 3
        lon_step = tap_index % 3
        shifted = jnp.roll(padded[lat_step:lat_step + row_count], 1 - lon_step, axis=1)
        summed = summed + jnp.dot(shifted.reshape(-1, channels), kernel[tap_index], preferred_element_type=jnp.float32)
    return summed.reshape(row_count, lon_count, -1)

def back_frame(frame, kernel):
    row_count, lon_count, channels = frame.shape
    padded = jnp.pad(frame, ((1, 1), (0, 0), (0, 0)))
    summed = jnp.zeros((row_count * lon_count, kernel.shape[1]), jnp.float32)
    for tap_index in range(9):
        lat_step = tap_index // 3
        lon_step = tap_index % 3
        shifted = jnp.roll(padded[2 - lat_step:2 - lat_step + row_count], lon_step - 1, axis=1)
        summed = summed + jnp.dot(shifted.reshape(-1, channels), kernel[tap_index].T, preferred_element_type=jnp.float32)
    return summed.reshape(row_count, lon_count, -1)

def reference(trajectory, cotangent, conv_weight, proj_weight, mixing, offsets):
    total_frames = trajectory.shape[0]
    channels = trajectory.shape[3]
    conv_out = lax.map(lambda frame: conv_frame(frame, conv_weight).astype(jnp.bfloat16), trajectory)
    frame_ids = jnp.arange(total_frames, dtype=jnp.int32)
    starts = jnp.clip(frame_ids - offsets, 0, total_frames - 5).astype(jnp.int32)
    places = (frame_ids - starts).astype(jnp.int32)

    def frame_grad(item):
        start_at, place_at, cot_frame = item
        window = lax.dynamic_slice_in_dim(conv_out, start_at, 5, 0).astype(jnp.float32)
        coeffs = lax.dynamic_slice_in_dim(mixing, (5 * place_at).astype(jnp.int32), 5, 0)
        pre = lax.optimization_barrier(jnp.sum(coeffs[:, None, None, :] * window, axis=0))
        g_hidden = jnp.dot(cot_frame.reshape(-1, channels), proj_weight.T, preferred_element_type=jnp.float32).reshape(pre.shape)
        return (g_hidden * silu_slope(pre)).astype(jnp.bfloat16)
    g_pre = lax.map(frame_grad, (starts, places, cotangent))

    def accumulate(carry, item):
        start_at, place_at, g_frame = item
        coeffs = lax.dynamic_slice_in_dim(mixing, (5 * place_at).astype(jnp.int32), 5, 0)
        block = lax.dynamic_slice_in_dim(carry, start_at, 5, 0)
        block = block + coeffs[:, None, None, :] * g_frame.astype(jnp.float32)[None]
        return (lax.dynamic_update_slice_in_dim(carry, block, start_at, 0), None)
    window_sum, _ = lax.scan(accumulate, jnp.zeros(trajectory.shape, jnp.float32), (starts, places, g_pre))
    conv_grad = window_sum.astype(jnp.bfloat16)

    def finish(pair):
        grad_frame, cot_frame = pair
        return (cot_frame.astype(jnp.float32) + back_frame(grad_frame, conv_weight)).astype(jnp.bfloat16)
    return lax.map(finish, (conv_grad, cotangent))
```

```python
import jax
import jax.numpy as jnp
from jax import lax
from jax.experimental import pallas as pl
from jax.experimental.pallas import tpu as pltpu
from jax.sharding import PartitionSpec as P

VMEM = pl.BlockSpec(memory_space=pltpu.VMEM)
SMEM = pl.BlockSpec(memory_space=pltpu.SMEM)
REACH = 4


def shift(value, axis, step):
    size = lax.axis_size(axis)
    return lax.ppermute(
        value, axis, [(i, i + step) for i in range(size) if 0 <= i + step < size]
    )


def taps(rows, weight_ref, transposed):
    summed = []
    for lon_tap in range(3):
        total = None
        for lat_tap in range(3):
            value = jnp.concatenate([r[lat_tap] for r in rows], axis=0)
            matrix = weight_ref[3 * lat_tap + lon_tap]
            term = lax.dot_general(
                value,
                matrix,
                (((1,), (1 if transposed else 0,)), ((), ())),
                preferred_element_type=jnp.float32,
            )
            total = term if total is None else total + term
        summed.append(total)
    return summed


def rolled(value, lon_count, step):
    split = value.reshape(-1, lon_count, value.shape[-1])
    return pltpu.roll(split, step % lon_count, axis=1).reshape(value.shape)


def flat(value):
    return value.reshape(-1, value.shape[-1])


def conv_kernel(x_ref, before_ref, after_ref, weight_ref, out_ref):
    frames, _, lon_count, channels = x_ref.shape
    first, second = flat(x_ref[:, 0]), flat(x_ref[:, 1])
    before, after = flat(before_ref[...]), flat(after_ref[...])
    low, mid, high = taps(
        [(before, first, second), (first, second, after)], weight_ref, False
    )
    total = mid + rolled(low, lon_count, 1) + rolled(high, lon_count, -1)
    total = total.astype(out_ref.dtype).reshape(2, frames, lon_count, channels)
    out_ref[:, 0] = total[0]
    out_ref[:, 1] = total[1]


def back_kernel(x_ref, before_ref, after_ref, weight_ref, cot_ref, out_ref):
    frames, _, lon_count, channels = x_ref.shape
    first, second = flat(x_ref[:, 0]), flat(x_ref[:, 1])
    before, after = flat(before_ref[...]), flat(after_ref[...])
    low, mid, high = taps(
        [(second, first, before), (after, second, first)], weight_ref, True
    )
    total = mid + rolled(low, lon_count, -1) + rolled(high, lon_count, 1)
    total = total.reshape(2, frames, lon_count, channels)
    for row in range(2):
        out_ref[:, row] = (cot_ref[:, row].astype(jnp.float32) + total[row]).astype(out_ref.dtype)


def start_of(offsets_ref, frame):
    total_frames = offsets_ref.shape[0]
    inside = jnp.clip(frame, 0, total_frames - 1)
    return jnp.clip(inside - offsets_ref[inside], 0, total_frames - 5)


def mid_kernel(offsets_ref, mixing_ref, left_ref, own_ref, right_ref, cot_ref, proj_ref, out_ref, near_ref):
    frames, row_count, lon_count, channels = own_ref.shape
    first_frame = lax.axis_index("tm") * frames
    near_ref[:REACH] = left_ref[...]
    near_ref[REACH : REACH + frames] = own_ref[...]
    near_ref[REACH + frames :] = right_ref[...]
    hidden = lax.dot_general(
        flat(cot_ref[...]), proj_ref[...], (((1,), (1,)), ((), ())), preferred_element_type=jnp.float32
    ).reshape(own_ref.shape)
    for frame in range(frames):
        start = start_of(offsets_ref, first_frame + frame)
        place = first_frame + frame - start
        base = start - first_frame + REACH
        for row in range(row_count):
            pre = jnp.zeros((lon_count, channels), jnp.float32)
            for j in range(5):
                weight = mixing_ref[pl.ds(5 * place + j, 1), :]
                pre = pre + weight * near_ref[base + j, row].astype(jnp.float32)
            sigma = jax.nn.sigmoid(pre)
            slope = sigma * (1.0 + pre * (1.0 - sigma))
            out_ref[frame, row] = (hidden[frame, row] * slope).astype(out_ref.dtype)


def sum_kernel(offsets_ref, mixing_ref, left_ref, own_ref, right_ref, out_ref, top_ref, bottom_ref):
    frames, row_count, lon_count, channels = own_ref.shape
    first_frame = lax.axis_index("tm") * frames
    total_frames = offsets_ref.shape[0]
    starts = [start_of(offsets_ref, first_frame + k - REACH) for k in range(frames + 2 * REACH)]
    for frame in range(frames):
        weights = []
        for k in range(frame, frame + 2 * REACH + 1):
            source = first_frame + k - REACH
            slot = first_frame + frame - starts[k]
            good = (slot >= 0) & (slot <= 4) & (source >= 0) & (source < total_frames)
            place = source - starts[k]
            row_id = jnp.where(good, 5 * place + slot, 0)
            weight = mixing_ref[pl.ds(row_id, 1), :]
            weights.append((k, jnp.where(good, weight, 0.0)))
        for row in range(row_count):
            total = jnp.zeros((lon_count, channels), jnp.float32)
            for k, weight in weights:
                if k < REACH:
                    value = left_ref[k, row]
                elif k < REACH + frames:
                    value = own_ref[k - REACH, row]
                else:
                    value = right_ref[k - REACH - frames, row]
                total = total + weight * value.astype(jnp.float32)
            rounded = total.astype(out_ref.dtype)
            out_ref[frame, row] = rounded
            if row == 0:
                top_ref[frame] = rounded
            if row == row_count - 1:
                bottom_ref[frame] = rounded


def call(kernel, out_shapes, specs, cost, **extra):
    return pl.pallas_call(
        kernel,
        out_shape=out_shapes,
        in_specs=specs,
        out_specs=jax.tree.map(lambda _: VMEM, out_shapes),
        compiler_params=pltpu.CompilerParams(vmem_limit_bytes=40 * 1024 * 1024),
        cost_estimate=pl.CostEstimate(flops=cost[0], bytes_accessed=cost[1], transcendentals=0),
        **extra,
    )


def body(trajectory, cotangent, conv_weight, proj_weight, mixing, offsets):
    frames, row_count, lon_count, channels = trajectory.shape
    block = jax.ShapeDtypeStruct(trajectory.shape, jnp.bfloat16)
    edge = jax.ShapeDtypeStruct((frames, lon_count, channels), jnp.bfloat16)
    conv_cost = (2 * 9 * frames * row_count * lon_count * channels * channels, 2_000_000)
    before = shift(trajectory[:, row_count - 1], "lat", 1)
    after = shift(trajectory[:, 0], "lat", -1)
    conv_out = call(conv_kernel, block, [VMEM] * 4, conv_cost)(trajectory, before, after, conv_weight)
    left, right = shift(conv_out, "tm", 1), shift(conv_out, "tm", -1)
    g_pre = call(
        mid_kernel, block, [SMEM] + [VMEM] * 6, (80_000_000, 1_400_000),
        scratch_shapes=[pltpu.VMEM((frames + 2 * REACH, row_count, lon_count, channels), jnp.bfloat16)],
    )(offsets, mixing, left, conv_out, right, cotangent, proj_weight)
    left, right = shift(g_pre, "tm", 1), shift(g_pre, "tm", -1)
    conv_grad, top, bottom = call(
        sum_kernel, (block, edge, edge), [SMEM] + [VMEM] * 4, (10_000_000, 1_400_000)
    )(offsets, mixing, left, g_pre, right)
    before, after = shift(bottom, "lat", 1), shift(top, "lat", -1)
    return call(back_kernel, block, [VMEM] * 5, conv_cost)(conv_grad, before, after, conv_weight, cotangent)


def solution(mesh):
    in_specs = (P("tm", "lat", None, None), P("tm", "lat", None, None), P(), P(), P(), P())
    out_specs = P("tm", "lat", None, None)
    return jax.shard_map(body, mesh=mesh, in_specs=in_specs, out_specs=out_specs, check_vma=False)
```

```python
import functools

import jax
import jax.numpy as jnp
from jax import lax
from jax.experimental import pallas as pl
from jax.experimental.pallas import tpu as pltpu
from jax.sharding import PartitionSpec as P

VMEM = pl.BlockSpec(memory_space=pltpu.VMEM)
SMEM = pl.BlockSpec(memory_space=pltpu.SMEM)
REACH = 4


def shift(value, axis, step):
    size = lax.axis_size(axis)
    return lax.ppermute(
        value, axis, [(i, i + step) for i in range(size) if 0 <= i + step < size]
    )


def swap(value, axis, offset):
    size = lax.axis_size(axis)
    pairs = [(i, i + 1) for i in range(offset, size - 1, 2)]
    return lax.ppermute(value, axis, pairs + [(j, i) for i, j in pairs])


def product(value, matrix, transposed):
    return lax.dot_general(
        value,
        matrix,
        (((1,), (1 if transposed else 0,)), ((), ())),
        preferred_element_type=jnp.float32,
    )


def rolled(value, lon_count, step):
    split = value.reshape(-1, lon_count, value.shape[-1])
    return pltpu.roll(split, step % lon_count, axis=1).reshape(value.shape)


def aligned(low, mid, high, lon_count, transposed):
    step = -1 if transposed else 1
    return mid + rolled(low, lon_count, step) + rolled(high, lon_count, -step)


def flat(value):
    return value.reshape(-1, value.shape[-1])


def local_kernel(transposed, x_ref, weight_ref, *refs):
    total_ref = refs[-1]
    lon_count = x_ref.shape[2]
    first, second = flat(x_ref[:, 0]), flat(x_ref[:, 1])
    half = first.shape[0]
    both = jnp.concatenate([first, second], axis=0)
    ahead, behind = (0, 2) if transposed else (2, 0)
    sums = [[], []]
    for lon_tap in range(3):
        middle = product(both, weight_ref[3 + lon_tap], transposed)
        sums[0].append(middle[:half] + product(second, weight_ref[3 * ahead + lon_tap], transposed))
        sums[1].append(middle[half:] + product(first, weight_ref[3 * behind + lon_tap], transposed))
    for row in range(2):
        total = aligned(*sums[row], lon_count, transposed)
        if transposed:
            total = total + flat(refs[0][:, row]).astype(jnp.float32)
        total_ref[row] = total


def halo_kernel(transposed, total_ref, far_ref, near_ref, weight_ref, out_ref):
    frames, lon_count, channels = far_ref.shape
    parity = lax.rem(lax.axis_index("lat"), 2)
    for row, edge_ref in ((1 - parity, near_ref), (parity, far_ref)):
        tap = 2 - 2 * row if transposed else 2 * row
        value = flat(edge_ref[...])
        parts = [product(value, weight_ref[3 * tap + lon_tap], transposed) for lon_tap in range(3)]
        total = total_ref[row] + aligned(*parts, lon_count, transposed)
        out_ref[:, row] = total.astype(out_ref.dtype).reshape(frames, lon_count, channels)


def start_of(offsets_ref, frame):
    total_frames = offsets_ref.shape[0]
    inside = jnp.clip(frame, 0, total_frames - 1)
    return jnp.clip(inside - offsets_ref[inside], 0, total_frames - 5)


def mid_kernel(offsets_ref, mixing_ref, left_ref, own_ref, right_ref, cot_ref, proj_ref, out_ref, near_ref):
    frames, row_count, lon_count, channels = own_ref.shape
    first_frame = lax.axis_index("tm") * frames
    near_ref[:REACH] = left_ref[...]
    near_ref[REACH : REACH + frames] = own_ref[...]
    near_ref[REACH + frames :] = right_ref[...]
    hidden = lax.dot_general(
        flat(cot_ref[...]), proj_ref[...], (((1,), (1,)), ((), ())), preferred_element_type=jnp.float32
    ).reshape(own_ref.shape)
    for frame in range(frames):
        start = start_of(offsets_ref, first_frame + frame)
        place = first_frame + frame - start
        base = start - first_frame + REACH
        for row in range(row_count):
            pre = jnp.zeros((lon_count, channels), jnp.float32)
            for j in range(5):
                weight = mixing_ref[pl.ds(5 * place + j, 1), :]
                pre = pre + weight * near_ref[base + j, row].astype(jnp.float32)
            sigma = jax.nn.sigmoid(pre)
            slope = sigma * (1.0 + pre * (1.0 - sigma))
            out_ref[frame, row] = (hidden[frame, row] * slope).astype(out_ref.dtype)


def sum_kernel(offsets_ref, mixing_ref, left_ref, own_ref, right_ref, out_ref, far_ref, near_ref):
    frames, row_count, lon_count, channels = own_ref.shape
    first_frame = lax.axis_index("tm") * frames
    total_frames = offsets_ref.shape[0]
    starts = [start_of(offsets_ref, first_frame + k - REACH) for k in range(frames + 2 * REACH)]
    for frame in range(frames):
        weights = []
        for k in range(frame, frame + 2 * REACH + 1):
            source = first_frame + k - REACH
            slot = first_frame + frame - starts[k]
            good = (slot >= 0) & (slot <= 4) & (source >= 0) & (source < total_frames)
            place = source - starts[k]
            row_id = jnp.where(good, 5 * place + slot, 0)
            weight = mixing_ref[pl.ds(row_id, 1), :]
            weights.append((k, jnp.where(good, weight, 0.0)))
        for row in range(row_count):
            total = jnp.zeros((lon_count, channels), jnp.float32)
            for k, weight in weights:
                if k < REACH:
                    value = left_ref[k, row]
                elif k < REACH + frames:
                    value = own_ref[k - REACH, row]
                else:
                    value = right_ref[k - REACH - frames, row]
                total = total + weight * value.astype(jnp.float32)
            out_ref[frame, row] = total.astype(out_ref.dtype)
    parity = lax.rem(lax.axis_index("lat"), 2)
    far_ref[...] = out_ref[:, parity]
    near_ref[...] = out_ref[:, 1 - parity]


def call(kernel, out_shapes, specs, cost, **extra):
    return pl.pallas_call(
        kernel,
        out_shape=out_shapes,
        in_specs=specs,
        out_specs=jax.tree.map(lambda _: VMEM, out_shapes),
        compiler_params=pltpu.CompilerParams(vmem_limit_bytes=24 * 1024 * 1024),
        cost_estimate=pl.CostEstimate(flops=cost[0], bytes_accessed=cost[1], transcendentals=0),
        **extra,
    )


def convolve(block, far, near, weight, transposed, *added):
    frames, row_count, lon_count, channels = block.shape
    half = 2 * 3 * frames * row_count * lon_count * channels * channels
    sums = jax.ShapeDtypeStruct((row_count, frames * lon_count, channels), jnp.float32)
    total = call(
        functools.partial(local_kernel, transposed), sums, [VMEM] * (2 + len(added)), (2 * half, 2_000_000)
    )(block, weight, *added)
    far, near = swap(far, "lat", 1), swap(near, "lat", 0)
    result = jax.ShapeDtypeStruct(block.shape, jnp.bfloat16)
    return call(functools.partial(halo_kernel, transposed), result, [VMEM] * 4, (half, 2_000_000))(
        total, far, near, weight
    )


def body(trajectory, cotangent, conv_weight, proj_weight, mixing, offsets):
    frames, row_count, lon_count, channels = trajectory.shape
    block = jax.ShapeDtypeStruct(trajectory.shape, jnp.bfloat16)
    edge = jax.ShapeDtypeStruct((frames, lon_count, channels), jnp.bfloat16)
    odd = lax.rem(lax.axis_index("lat"), 2) == 1
    top, bottom = trajectory[:, 0], trajectory[:, 1]
    far, near = jnp.where(odd, bottom, top), jnp.where(odd, top, bottom)
    conv_out = convolve(trajectory, far, near, conv_weight, False)
    right, left = shift(conv_out, "tm", -1), shift(conv_out, "tm", 1)
    g_pre = call(
        mid_kernel, block, [SMEM] + [VMEM] * 6, (80_000_000, 1_400_000),
        scratch_shapes=[pltpu.VMEM((frames + 2 * REACH, row_count, lon_count, channels), jnp.bfloat16)],
    )(offsets, mixing, left, conv_out, right, cotangent, proj_weight)
    right, left = shift(g_pre, "tm", -1), shift(g_pre, "tm", 1)
    conv_grad, far, near = call(
        sum_kernel, (block, edge, edge), [SMEM] + [VMEM] * 4, (10_000_000, 1_400_000)
    )(offsets, mixing, left, g_pre, right)
    return convolve(conv_grad, far, near, conv_weight, True, cotangent)


def solution(mesh):
    in_specs = (P("tm", "lat", None, None), P("tm", "lat", None, None), P(), P(), P(), P())
    out_specs = P("tm", "lat", None, None)
    return jax.shard_map(body, mesh=mesh, in_specs=in_specs, out_specs=out_specs, check_vma=False)
```

```python
import functools

import jax
import jax.numpy as jnp
from jax import lax
from jax.experimental import pallas as pl
from jax.experimental.pallas import tpu as pltpu
from jax.sharding import PartitionSpec as P

VMEM = pl.BlockSpec(memory_space=pltpu.VMEM)
SMEM = pl.BlockSpec(memory_space=pltpu.SMEM)
REACH = 4


def swap(value, axis, offset):
    size = lax.axis_size(axis)
    pairs = [(i, i + 1) for i in range(offset, size - 1, 2)]
    return lax.ppermute(value, axis, pairs + [(j, i) for i, j in pairs])


def product(value, matrix, transposed):
    return lax.dot_general(
        value,
        matrix,
        (((1,), (1 if transposed else 0,)), ((), ())),
        preferred_element_type=jnp.float32,
    )


def rolled(value, lon_count, step):
    split = value.reshape(-1, lon_count, value.shape[-1])
    return pltpu.roll(split, step % lon_count, axis=1).reshape(value.shape)


def aligned(low, mid, high, lon_count, transposed):
    step = -1 if transposed else 1
    return mid + rolled(low, lon_count, step) + rolled(high, lon_count, -step)


def flat(value):
    return value.reshape(-1, value.shape[-1])


def local_kernel(transposed, x_ref, weight_ref, *refs):
    total_ref = refs[-1]
    lon_count = x_ref.shape[2]
    first, second = flat(x_ref[:, 0]), flat(x_ref[:, 1])
    half = first.shape[0]
    both = jnp.concatenate([first, second], axis=0)
    ahead, behind = (0, 2) if transposed else (2, 0)
    sums = [[], []]
    for lon_tap in range(3):
        middle = product(both, weight_ref[3 + lon_tap], transposed)
        sums[0].append(middle[:half] + product(second, weight_ref[3 * ahead + lon_tap], transposed))
        sums[1].append(middle[half:] + product(first, weight_ref[3 * behind + lon_tap], transposed))
    for row in range(2):
        total = aligned(*sums[row], lon_count, transposed)
        if transposed:
            total = total + flat(refs[0][:, row]).astype(jnp.float32)
        total_ref[row] = total


def halo_kernel(transposed, total_ref, far_ref, near_ref, weight_ref, out_ref):
    frames, lon_count, channels = far_ref.shape
    parity = lax.rem(lax.axis_index("lat"), 2)
    for row, edge_ref in ((1 - parity, near_ref), (parity, far_ref)):
        tap = 2 - 2 * row if transposed else 2 * row
        value = flat(edge_ref[...])
        parts = [product(value, weight_ref[3 * tap + lon_tap], transposed) for lon_tap in range(3)]
        total = total_ref[row] + aligned(*parts, lon_count, transposed)
        out_ref[:, row] = total.astype(out_ref.dtype).reshape(frames, lon_count, channels)


def start_of(offsets_ref, frame):
    total_frames = offsets_ref.shape[0]
    inside = jnp.clip(frame, 0, total_frames - 1)
    return jnp.clip(inside - offsets_ref[inside], 0, total_frames - 5)


def gather(odd_ref, own_ref, even_ref, near_ref):
    frames = own_ref.shape[0]
    parity = lax.rem(lax.axis_index("tm"), 2)
    span = REACH + frames
    near_ref[pl.ds(span * parity, frames)] = odd_ref[...]
    near_ref[REACH:span] = own_ref[...]
    near_ref[pl.ds(span * (1 - parity), frames)] = even_ref[...]


def mid_kernel(offsets_ref, mixing_ref, odd_ref, own_ref, even_ref, cot_ref, proj_ref, out_ref, near_ref):
    frames, row_count, lon_count, channels = own_ref.shape
    first_frame = lax.axis_index("tm") * frames
    gather(odd_ref, own_ref, even_ref, near_ref)
    hidden = lax.dot_general(
        flat(cot_ref[...]), proj_ref[...], (((1,), (1,)), ((), ())), preferred_element_type=jnp.float32
    ).reshape(own_ref.shape)
    for frame in range(frames):
        start = start_of(offsets_ref, first_frame + frame)
        place = first_frame + frame - start
        base = start - first_frame + REACH
        for row in range(row_count):
            pre = jnp.zeros((lon_count, channels), jnp.float32)
            for j in range(5):
                weight = mixing_ref[pl.ds(5 * place + j, 1), :]
                pre = pre + weight * near_ref[base + j, row].astype(jnp.float32)
            sigma = jax.nn.sigmoid(pre)
            slope = sigma * (1.0 + pre * (1.0 - sigma))
            out_ref[frame, row] = (hidden[frame, row] * slope).astype(out_ref.dtype)


def cut_kernel(x_ref, far_ref, near_ref):
    parity = lax.rem(lax.axis_index("lat"), 2)
    far_ref[...] = x_ref[:, parity]
    near_ref[...] = x_ref[:, 1 - parity]


def sum_kernel(offsets_ref, mixing_ref, odd_ref, own_ref, even_ref, out_ref, far_ref, near_ref, span_ref):
    frames, row_count, lon_count, channels = own_ref.shape
    gather(odd_ref, own_ref, even_ref, span_ref)
    first_frame = lax.axis_index("tm") * frames
    total_frames = offsets_ref.shape[0]
    starts = [start_of(offsets_ref, first_frame + k - REACH) for k in range(frames + 2 * REACH)]
    for frame in range(frames):
        weights = []
        for k in range(frame, frame + 2 * REACH + 1):
            source = first_frame + k - REACH
            slot = first_frame + frame - starts[k]
            good = (slot >= 0) & (slot <= 4) & (source >= 0) & (source < total_frames)
            place = source - starts[k]
            row_id = jnp.where(good, 5 * place + slot, 0)
            weight = mixing_ref[pl.ds(row_id, 1), :]
            weights.append((k, jnp.where(good, weight, 0.0)))
        for row in range(row_count):
            total = jnp.zeros((lon_count, channels), jnp.float32)
            for k, weight in weights:
                value = span_ref[k, row]
                total = total + weight * value.astype(jnp.float32)
            out_ref[frame, row] = total.astype(out_ref.dtype)
    parity = lax.rem(lax.axis_index("lat"), 2)
    far_ref[...] = out_ref[:, parity]
    near_ref[...] = out_ref[:, 1 - parity]


def call(kernel, out_shapes, specs, cost, **extra):
    return pl.pallas_call(
        kernel,
        out_shape=out_shapes,
        in_specs=specs,
        out_specs=jax.tree.map(lambda _: VMEM, out_shapes),
        compiler_params=pltpu.CompilerParams(vmem_limit_bytes=24 * 1024 * 1024),
        cost_estimate=pl.CostEstimate(flops=cost[0], bytes_accessed=cost[1], transcendentals=0),
        **extra,
    )


def convolve(block, far, near, weight, transposed, *added):
    frames, row_count, lon_count, channels = block.shape
    half = 2 * 3 * frames * row_count * lon_count * channels * channels
    sums = jax.ShapeDtypeStruct((row_count, frames * lon_count, channels), jnp.float32)
    total = call(
        functools.partial(local_kernel, transposed), sums, [VMEM] * (2 + len(added)), (2 * half, 2_000_000)
    )(block, weight, *added)
    far, near = swap(far, "lat", 1), swap(near, "lat", 0)
    result = jax.ShapeDtypeStruct(block.shape, jnp.bfloat16)
    return call(functools.partial(halo_kernel, transposed), result, [VMEM] * 4, (half, 2_000_000))(
        total, far, near, weight
    )


def body(trajectory, cotangent, conv_weight, proj_weight, mixing, offsets):
    frames, row_count, lon_count, channels = trajectory.shape
    block = jax.ShapeDtypeStruct(trajectory.shape, jnp.bfloat16)
    edge = jax.ShapeDtypeStruct((frames, lon_count, channels), jnp.bfloat16)
    far, near = call(cut_kernel, (edge, edge), [VMEM], (1_000, 600_000))(trajectory)
    scratch = [pltpu.VMEM((frames + 2 * REACH, row_count, lon_count, channels), jnp.bfloat16)]
    conv_out = convolve(trajectory, far, near, conv_weight, False)
    odd, even = swap(conv_out, "tm", 1), swap(conv_out, "tm", 0)
    g_pre = call(
        mid_kernel, block, [SMEM] + [VMEM] * 6, (80_000_000, 1_400_000),
        scratch_shapes=scratch,
    )(offsets, mixing, odd, conv_out, even, cotangent, proj_weight)
    odd, even = swap(g_pre, "tm", 1), swap(g_pre, "tm", 0)
    conv_grad, far, near = call(
        sum_kernel, (block, edge, edge), [SMEM] + [VMEM] * 4, (10_000_000, 1_400_000), scratch_shapes=scratch
    )(offsets, mixing, odd, g_pre, even)
    return convolve(conv_grad, far, near, conv_weight, True, cotangent)


def solution(mesh):
    in_specs = (P("tm", "lat", None, None), P("tm", "lat", None, None), P(), P(), P(), P())
    out_specs = P("tm", "lat", None, None)
    return jax.shard_map(body, mesh=mesh, in_specs=in_specs, out_specs=out_specs, check_vma=False)
```

```python
import functools

import jax
import jax.numpy as jnp
from jax import lax
from jax.experimental import pallas as pl
from jax.experimental.pallas import tpu as pltpu
from jax.sharding import PartitionSpec as P

VMEM = pl.BlockSpec(memory_space=pltpu.VMEM)
SMEM = pl.BlockSpec(memory_space=pltpu.SMEM)
REACH = 4


def swap(value, axis, offset):
    size = lax.axis_size(axis)
    pairs = [(i, i + 1) for i in range(offset, size - 1, 2)]
    return lax.ppermute(value, axis, pairs + [(j, i) for i, j in pairs])


def crossed(value, turn):
    frames, bands = lax.axis_size("tm"), lax.axis_size("lat")
    pairs = []
    for band in range(bands):
        for i in range((band + turn) % 2, frames - 1, 2):
            pairs.append((i * bands + band, (i + 1) * bands + band))
    return lax.ppermute(value, ("tm", "lat"), pairs + [(j, i) for i, j in pairs])


def product(value, matrix, transposed):
    return lax.dot_general(
        value,
        matrix,
        (((1,), (1 if transposed else 0,)), ((), ())),
        preferred_element_type=jnp.float32,
    )


def rolled(value, lon_count, step):
    split = value.reshape(-1, lon_count, value.shape[-1])
    return pltpu.roll(split, step % lon_count, axis=1).reshape(value.shape)


def aligned(low, mid, high, lon_count, transposed):
    step = -1 if transposed else 1
    return mid + rolled(low, lon_count, step) + rolled(high, lon_count, -step)


def flat(value):
    return value.reshape(-1, value.shape[-1])


def local_kernel(transposed, x_ref, weight_ref, *refs):
    total_ref = refs[-1]
    lon_count = x_ref.shape[2]
    first, second = flat(x_ref[:, 0]), flat(x_ref[:, 1])
    half = first.shape[0]
    both = jnp.concatenate([first, second], axis=0)
    ahead, behind = (0, 2) if transposed else (2, 0)
    sums = [[], []]
    for lon_tap in range(3):
        middle = product(both, weight_ref[3 + lon_tap], transposed)
        sums[0].append(middle[:half] + product(second, weight_ref[3 * ahead + lon_tap], transposed))
        sums[1].append(middle[half:] + product(first, weight_ref[3 * behind + lon_tap], transposed))
    for row in range(2):
        total = aligned(*sums[row], lon_count, transposed)
        if transposed:
            total = total + flat(refs[0][:, row]).astype(jnp.float32)
        total_ref[row] = total


def halo_kernel(transposed, total_ref, far_ref, near_ref, weight_ref, out_ref):
    frames, lon_count, channels = far_ref.shape
    parity = lax.rem(lax.axis_index("lat"), 2)
    for row, edge_ref in ((1 - parity, near_ref), (parity, far_ref)):
        tap = 2 - 2 * row if transposed else 2 * row
        value = flat(edge_ref[...])
        parts = [product(value, weight_ref[3 * tap + lon_tap], transposed) for lon_tap in range(3)]
        total = total_ref[row] + aligned(*parts, lon_count, transposed)
        out_ref[:, row] = total.astype(out_ref.dtype).reshape(frames, lon_count, channels)


def start_of(offsets_ref, frame):
    total_frames = offsets_ref.shape[0]
    inside = jnp.clip(frame, 0, total_frames - 1)
    return jnp.clip(inside - offsets_ref[inside], 0, total_frames - 5)


def gather(first_ref, own_ref, second_ref, near_ref):
    frames = own_ref.shape[0]
    side = lax.rem(lax.axis_index("tm") + lax.axis_index("lat"), 2)
    span = REACH + frames
    near_ref[pl.ds(span * (1 - side), frames)] = first_ref[...]
    near_ref[REACH:span] = own_ref[...]
    near_ref[pl.ds(span * side, frames)] = second_ref[...]


def mid_kernel(offsets_ref, mixing_ref, second_ref, own_ref, first_ref, cot_ref, proj_ref, out_ref, near_ref):
    frames, row_count, lon_count, channels = own_ref.shape
    first_frame = lax.axis_index("tm") * frames
    gather(first_ref, own_ref, second_ref, near_ref)
    hidden = lax.dot_general(
        flat(cot_ref[...]), proj_ref[...], (((1,), (1,)), ((), ())), preferred_element_type=jnp.float32
    ).reshape(own_ref.shape)
    for frame in range(frames):
        start = start_of(offsets_ref, first_frame + frame)
        place = first_frame + frame - start
        base = start - first_frame + REACH
        for row in range(row_count):
            pre = jnp.zeros((lon_count, channels), jnp.float32)
            for j in range(5):
                weight = mixing_ref[pl.ds(5 * place + j, 1), :]
                pre = pre + weight * near_ref[base + j, row].astype(jnp.float32)
            sigma = jax.nn.sigmoid(pre)
            slope = sigma * (1.0 + pre * (1.0 - sigma))
            out_ref[frame, row] = (hidden[frame, row] * slope).astype(out_ref.dtype)


def cut_kernel(x_ref, far_ref, near_ref):
    parity = lax.rem(lax.axis_index("lat"), 2)
    far_ref[...] = x_ref[:, parity]
    near_ref[...] = x_ref[:, 1 - parity]


def sum_kernel(offsets_ref, mixing_ref, second_ref, own_ref, first_ref, out_ref, far_ref, near_ref, span_ref):
    frames, row_count, lon_count, channels = own_ref.shape
    gather(first_ref, own_ref, second_ref, span_ref)
    first_frame = lax.axis_index("tm") * frames
    total_frames = offsets_ref.shape[0]
    starts = [start_of(offsets_ref, first_frame + k - REACH) for k in range(frames + 2 * REACH)]
    for frame in range(frames):
        weights = []
        for k in range(frame, frame + 2 * REACH + 1):
            source = first_frame + k - REACH
            slot = first_frame + frame - starts[k]
            good = (slot >= 0) & (slot <= 4) & (source >= 0) & (source < total_frames)
            place = source - starts[k]
            row_id = jnp.where(good, 5 * place + slot, 0)
            weight = mixing_ref[pl.ds(row_id, 1), :]
            weights.append((k, jnp.where(good, weight, 0.0)))
        for row in range(row_count):
            total = jnp.zeros((lon_count, channels), jnp.float32)
            for k, weight in weights:
                value = span_ref[k, row]
                total = total + weight * value.astype(jnp.float32)
            out_ref[frame, row] = total.astype(out_ref.dtype)
    parity = lax.rem(lax.axis_index("lat"), 2)
    far_ref[...] = out_ref[:, parity]
    near_ref[...] = out_ref[:, 1 - parity]


def call(kernel, out_shapes, specs, cost, **extra):
    return pl.pallas_call(
        kernel,
        out_shape=out_shapes,
        in_specs=specs,
        out_specs=jax.tree.map(lambda _: VMEM, out_shapes),
        compiler_params=pltpu.CompilerParams(vmem_limit_bytes=24 * 1024 * 1024),
        cost_estimate=pl.CostEstimate(flops=cost[0], bytes_accessed=cost[1], transcendentals=0),
        **extra,
    )


def convolve(block, far, near, weight, transposed, *added):
    frames, row_count, lon_count, channels = block.shape
    half = 2 * 3 * frames * row_count * lon_count * channels * channels
    sums = jax.ShapeDtypeStruct((row_count, frames * lon_count, channels), jnp.float32)
    total = call(
        functools.partial(local_kernel, transposed), sums, [VMEM] * (2 + len(added)), (2 * half, 2_000_000)
    )(block, weight, *added)
    far, near = swap(far, "lat", 1), swap(near, "lat", 0)
    result = jax.ShapeDtypeStruct(block.shape, jnp.bfloat16)
    return call(functools.partial(halo_kernel, transposed), result, [VMEM] * 4, (half, 2_000_000))(
        total, far, near, weight
    )


def body(trajectory, cotangent, conv_weight, proj_weight, mixing, offsets):
    frames, row_count, lon_count, channels = trajectory.shape
    block = jax.ShapeDtypeStruct(trajectory.shape, jnp.bfloat16)
    edge = jax.ShapeDtypeStruct((frames, lon_count, channels), jnp.bfloat16)
    far, near = call(cut_kernel, (edge, edge), [VMEM], (1_000, 600_000))(trajectory)
    scratch = [pltpu.VMEM((frames + 2 * REACH, row_count, lon_count, channels), jnp.bfloat16)]
    conv_out = convolve(trajectory, far, near, conv_weight, False)
    first, second = crossed(conv_out, 0), crossed(conv_out, 1)
    g_pre = call(
        mid_kernel, block, [SMEM] + [VMEM] * 6, (80_000_000, 1_400_000),
        scratch_shapes=scratch,
    )(offsets, mixing, second, conv_out, first, cotangent, proj_weight)
    first, second = crossed(g_pre, 0), crossed(g_pre, 1)
    conv_grad, far, near = call(
        sum_kernel, (block, edge, edge), [SMEM] + [VMEM] * 4, (10_000_000, 1_400_000), scratch_shapes=scratch
    )(offsets, mixing, second, g_pre, first)
    return convolve(conv_grad, far, near, conv_weight, True, cotangent)


def solution(mesh):
    in_specs = (P("tm", "lat", None, None), P("tm", "lat", None, None), P(), P(), P(), P())
    out_specs = P("tm", "lat", None, None)
    return jax.shard_map(body, mesh=mesh, in_specs=in_specs, out_specs=out_specs, check_vma=False)
```

```python
import functools

import jax
import jax.numpy as jnp
from jax import lax
from jax.experimental import pallas as pl
from jax.experimental.pallas import tpu as pltpu
from jax.sharding import PartitionSpec as P

VMEM = pl.BlockSpec(memory_space=pltpu.VMEM)
SMEM = pl.BlockSpec(memory_space=pltpu.SMEM)
REACH = 4


def swap(value, axis, offset):
    size = lax.axis_size(axis)
    pairs = [(i, i + 1) for i in range(offset, size - 1, 2)]
    return lax.ppermute(value, axis, pairs + [(j, i) for i, j in pairs])


def crossed(value, turn):
    frames, bands = lax.axis_size("tm"), lax.axis_size("lat")
    pairs = []
    for band in range(bands):
        for i in range((band + turn) % 2, frames - 1, 2):
            pairs.append((i * bands + band, (i + 1) * bands + band))
    return lax.ppermute(value, ("tm", "lat"), pairs + [(j, i) for i, j in pairs])


def product(value, matrix, transposed):
    return lax.dot_general(
        value,
        matrix,
        (((1,), (1 if transposed else 0,)), ((), ())),
        preferred_element_type=jnp.float32,
    )


def rolled(value, lon_count, step):
    split = value.reshape(-1, lon_count, value.shape[-1])
    return pltpu.roll(split, step % lon_count, axis=1).reshape(value.shape)


def aligned(low, mid, high, lon_count, transposed):
    step = -1 if transposed else 1
    return mid + rolled(low, lon_count, step) + rolled(high, lon_count, -step)


def flat(value):
    return value.reshape(-1, value.shape[-1])


def local_kernel(transposed, x_ref, weight_ref, *refs):
    total_ref = refs[-1]
    lon_count = x_ref.shape[2]
    first, second = flat(x_ref[:, 0]), flat(x_ref[:, 1])
    half = first.shape[0]
    both = jnp.concatenate([first, second], axis=0)
    ahead, behind = (0, 2) if transposed else (2, 0)
    sums = [[], []]
    for lon_tap in range(3):
        middle = product(both, weight_ref[3 + lon_tap], transposed)
        sums[0].append(middle[:half] + product(second, weight_ref[3 * ahead + lon_tap], transposed))
        sums[1].append(middle[half:] + product(first, weight_ref[3 * behind + lon_tap], transposed))
    for row in range(2):
        total_ref[row] = aligned(*sums[row], lon_count, transposed)


def halo_kernel(transposed, total_ref, far_ref, near_ref, weight_ref, out_ref):
    frames, lon_count, channels = far_ref.shape
    parity = lax.rem(lax.axis_index("lat"), 2)
    for row, edge_ref in ((1 - parity, near_ref), (parity, far_ref)):
        tap = 2 - 2 * row if transposed else 2 * row
        value = flat(edge_ref[...])
        parts = [product(value, weight_ref[3 * tap + lon_tap], transposed) for lon_tap in range(3)]
        total = total_ref[row] + aligned(*parts, lon_count, transposed)
        out_ref[:, row] = total.astype(out_ref.dtype).reshape(frames, lon_count, channels)


def start_of(offsets_ref, frame):
    total_frames = offsets_ref.shape[0]
    inside = jnp.clip(frame, 0, total_frames - 1)
    return jnp.clip(inside - offsets_ref[inside], 0, total_frames - 5)


def weight_of(offsets_ref, mixing_ref, frame, target):
    start = start_of(offsets_ref, frame)
    slot = target - start
    good = (slot >= 0) & (slot <= 4) & (frame >= 0) & (frame < offsets_ref.shape[0])
    weight = mixing_ref[pl.ds(jnp.where(good, 5 * (frame - start) + slot, 0), 1), :]
    return jnp.where(good, weight, 0.0)


LAGS = 2 * REACH + 1


def table_kernel(offsets_ref, mixing_ref, after_ref, reads_ref, read_by_ref):
    del after_ref
    frames = reads_ref.shape[0] // LAGS
    base = lax.axis_index("tm") * frames
    for frame in range(frames):
        for lag in range(-REACH, REACH + 1):
            row = frame * LAGS + lag + REACH
            here, there = base + frame, base + frame + lag
            reads_ref[row : row + 1, :] = weight_of(offsets_ref, mixing_ref, here, there)
            read_by_ref[row : row + 1, :] = weight_of(offsets_ref, mixing_ref, there, here)


def mixed(table_ref, sources, rows, total_of, store):
    frames = sources[0][0].shape[0]
    for frame in range(frames):
        for row in rows:
            total = total_of(frame, row)
            for ref, first in sources:
                for k in range(frames):
                    lag = first + k - frame
                    if abs(lag) <= REACH:
                        line = frame * LAGS + lag + REACH
                        term = table_ref[line : line + 1, :] * ref[k, row].astype(jnp.float32)
                        total = term if total is None else total + term
            store(frame, row, total)


def own_kernel(table_ref, own_ref, total_ref):
    def store(frame, row, total):
        total_ref[frame, row] = total

    mixed(table_ref, [(own_ref, 0)], range(2), lambda *_: None, store)


def sided(first_ref, second_ref, run):
    side = lax.rem(lax.axis_index("tm") + lax.axis_index("lat"), 2)

    @pl.when(side == 1)
    def _():
        run(first_ref, second_ref)

    @pl.when(side == 0)
    def _():
        run(second_ref, first_ref)


def mid_kernel(table_ref, second_ref, total_ref, first_ref, hidden_ref, out_ref):
    frames = out_ref.shape[0]

    def store(frame, row, pre):
        sigma = 0.5 + 0.5 * jnp.tanh(0.5 * pre)
        slope = sigma * (1.0 + pre * (1.0 - sigma))
        out_ref[frame, row] = (hidden_ref[frame, row] * slope).astype(out_ref.dtype)

    def run(before, after):
        sources = [(before, -frames), (after, frames)]
        mixed(table_ref, sources, range(2), lambda frame, row: total_ref[frame, row], store)

    sided(first_ref, second_ref, run)


def hidden_kernel(cot_ref, proj_ref, out_ref):
    out_ref[...] = product(flat(cot_ref[...]), proj_ref[...], True).reshape(out_ref.shape)


def cut_kernel(x_ref, far_ref, near_ref):
    parity = lax.rem(lax.axis_index("lat"), 2)
    far_ref[...] = x_ref[:, parity]
    near_ref[...] = x_ref[:, 1 - parity]


def sum_kernel(far, table_ref, second_ref, total_ref, first_ref, out_ref):
    frames = out_ref.shape[0]
    parity = lax.rem(lax.axis_index("lat"), 2)
    row = parity if far else 1 - parity

    def store(frame, _, total):
        out_ref[frame] = total.astype(out_ref.dtype)

    def run(before, after):
        sources = [(before, -frames), (after, frames)]
        mixed(table_ref, sources, [row], lambda frame, _: total_ref[frame, row], store)

    sided(first_ref, second_ref, run)


def back_local_kernel(far_ref, near_ref, weight_ref, cot_ref, far_total, near_total):
    lon_count = far_ref.shape[1]
    parity = lax.rem(lax.axis_index("lat"), 2)
    far, near = flat(far_ref[...]), flat(near_ref[...])
    half = near.shape[0]
    both = jnp.concatenate([far, near], axis=0)
    tap = 2 * parity
    far_sums, near_sums = [], []
    for lon_tap in range(3):
        middle = product(both, weight_ref[3 + lon_tap], True)
        far_sums.append(middle[:half] + product(near, weight_ref[3 * tap + lon_tap], True))
        near_sums.append(middle[half:] + product(far, weight_ref[3 * (2 - tap) + lon_tap], True))
    for row, sums, out_ref in ((parity, far_sums, far_total), (1 - parity, near_sums, near_total)):
        out_ref[...] = aligned(*sums, lon_count, True) + flat(cot_ref[:, row]).astype(jnp.float32)


def back_halo(tap, total_ref, halo_ref, weight_ref, out_ref):
    value = flat(halo_ref[...])
    parts = [product(value, weight_ref[3 * tap + lon_tap], True) for lon_tap in range(3)]
    total = total_ref[...] + aligned(*parts, halo_ref.shape[1], True)
    out_ref[...] = total.astype(out_ref.dtype).reshape(out_ref.shape)


def final_kernel(far_total, far_halo, near_total, near_halo, weight_ref, out_ref, near_ref, far_ref, sems):
    parity = lax.rem(lax.axis_index("lat"), 2)
    back_halo(2 * parity, near_total, near_halo, weight_ref, near_ref)
    near_copy = pltpu.make_async_copy(near_ref, out_ref.at[:, 1 - parity], sems.at[0])
    near_copy.start()
    back_halo(2 - 2 * parity, far_total, far_halo, weight_ref, far_ref)
    far_copy = pltpu.make_async_copy(far_ref, out_ref.at[:, parity], sems.at[1])
    far_copy.start()
    near_copy.wait()
    far_copy.wait()


def call(kernel, out_shapes, specs, cost, out_specs=None, **extra):
    return pl.pallas_call(
        kernel,
        out_shape=out_shapes,
        in_specs=specs,
        out_specs=out_specs or jax.tree.map(lambda _: VMEM, out_shapes),
        compiler_params=pltpu.CompilerParams(vmem_limit_bytes=24 * 1024 * 1024),
        cost_estimate=pl.CostEstimate(flops=cost[0], bytes_accessed=cost[1], transcendentals=0),
        **extra,
    )


def convolve(block, far, near, weight, transposed, *added):
    frames, row_count, lon_count, channels = block.shape
    half = 2 * 3 * frames * row_count * lon_count * channels * channels
    sums = jax.ShapeDtypeStruct((row_count, frames * lon_count, channels), jnp.float32)
    total = call(
        functools.partial(local_kernel, transposed), sums, [VMEM] * (2 + len(added)), (2 * half, 2_000_000)
    )(block, weight, *added)
    far, near = swap(far, "lat", 1), swap(near, "lat", 0)
    result = jax.ShapeDtypeStruct(block.shape, jnp.bfloat16)
    return call(functools.partial(halo_kernel, transposed), result, [VMEM] * 4, (half, 2_000_000))(
        total, far, near, weight
    )


def body(trajectory, cotangent, conv_weight, proj_weight, mixing, offsets):
    frames, row_count, lon_count, channels = trajectory.shape
    block = jax.ShapeDtypeStruct(trajectory.shape, jnp.bfloat16)
    edge = jax.ShapeDtypeStruct((frames, lon_count, channels), jnp.bfloat16)
    far, near = call(cut_kernel, (edge, edge), [VMEM], (4_000_000_000, 600_000))(trajectory)
    wide = jax.ShapeDtypeStruct(trajectory.shape, jnp.float32)
    conv_out = convolve(trajectory, far, near, conv_weight, False)
    table = jax.ShapeDtypeStruct((frames * LAGS, channels), jnp.float32)
    reads, read_by = call(table_kernel, (table, table), [SMEM] + [VMEM] * 2, (1_000_000, 200_000))(
        offsets, mixing, conv_out
    )
    first, second = crossed(conv_out, 0), crossed(conv_out, 1)
    hidden = call(hidden_kernel, wide, [VMEM] * 2, (67_000_000, 1_000_000))(cotangent, proj_weight)
    own = call(own_kernel, wide, [VMEM] * 2, (10_000_000, 1_000_000))(reads, conv_out)
    g_pre = call(mid_kernel, block, [VMEM] * 5, (10_000_000, 1_400_000))(reads, second, own, first, hidden)
    first, second = crossed(g_pre, 0), crossed(g_pre, 1)
    own = call(own_kernel, wide, [VMEM] * 2, (10_000_000, 1_000_000))(read_by, g_pre)
    far, near = [
        call(functools.partial(sum_kernel, is_far), edge, [VMEM] * 4, (5_000_000, 700_000))(
            read_by, second, own, first
        )
        for is_far in (True, False)
    ]
    far_halo, near_halo = swap(far, "lat", 1), swap(near, "lat", 0)
    tap = 2 * 3 * frames * lon_count * channels * channels
    sums = jax.ShapeDtypeStruct((frames * lon_count, channels), jnp.float32)
    far_total, near_total = call(back_local_kernel, (sums, sums), [VMEM] * 4, (4 * tap, 2_000_000))(
        far, near, conv_weight, cotangent
    )
    return call(
        final_kernel, block, [VMEM] * 5, (2 * tap, 2_000_000), out_specs=pl.BlockSpec(memory_space=pl.ANY),
        scratch_shapes=[pltpu.VMEM(edge.shape, edge.dtype)] * 2 + [pltpu.SemaphoreType.DMA((2,))],
    )(far_total, far_halo, near_total, near_halo, conv_weight)


def solution(mesh):
    in_specs = (P("tm", "lat", None, None), P("tm", "lat", None, None), P(), P(), P(), P())
    out_specs = P("tm", "lat", None, None)
    return jax.shard_map(body, mesh=mesh, in_specs=in_specs, out_specs=out_specs, check_vma=False)
```

```python
import functools

import jax
import jax.numpy as jnp
from jax import lax
from jax.experimental import pallas as pl
from jax.experimental.pallas import tpu as pltpu
from jax.sharding import PartitionSpec as P

VMEM = pl.BlockSpec(memory_space=pltpu.VMEM)
SMEM = pl.BlockSpec(memory_space=pltpu.SMEM)
REACH = 4


def swap(value, axis, offset):
    size = lax.axis_size(axis)
    pairs = [(i, i + 1) for i in range(offset, size - 1, 2)]
    return lax.ppermute(value, axis, pairs + [(j, i) for i, j in pairs])


def crossed(value, turn):
    frames, bands = lax.axis_size("tm"), lax.axis_size("lat")
    pairs = []
    for band in range(bands):
        for i in range((min(band, 1) + turn) % 2, frames - 1, 2):
            pairs.append((i * bands + band, (i + 1) * bands + band))
    return lax.ppermute(value, ("tm", "lat"), pairs + [(j, i) for i, j in pairs])


def product(value, matrix, transposed):
    return lax.dot_general(
        value,
        matrix,
        (((1,), (1 if transposed else 0,)), ((), ())),
        preferred_element_type=jnp.float32,
    )


def rolled(value, lon_count, step):
    split = value.reshape(-1, lon_count, value.shape[-1])
    return pltpu.roll(split, step % lon_count, axis=1).reshape(value.shape)


def aligned(low, mid, high, lon_count, transposed):
    step = -1 if transposed else 1
    return mid + rolled(low, lon_count, step) + rolled(high, lon_count, -step)


def flat(value):
    return value.reshape(-1, value.shape[-1])


def local_kernel(transposed, x_ref, weight_ref, *refs):
    total_ref = refs[-1]
    lon_count = x_ref.shape[2]
    first, second = flat(x_ref[:, 0]), flat(x_ref[:, 1])
    half = first.shape[0]
    both = jnp.concatenate([first, second], axis=0)
    ahead, behind = (0, 2) if transposed else (2, 0)
    sums = [[], []]
    for lon_tap in range(3):
        middle = product(both, weight_ref[3 + lon_tap], transposed)
        sums[0].append(middle[:half] + product(second, weight_ref[3 * ahead + lon_tap], transposed))
        sums[1].append(middle[half:] + product(first, weight_ref[3 * behind + lon_tap], transposed))
    for row in range(2):
        total_ref[row] = aligned(*sums[row], lon_count, transposed)


def halo_kernel(transposed, total_ref, far_ref, near_ref, weight_ref, out_ref):
    frames, lon_count, channels = far_ref.shape
    parity = lax.rem(lax.axis_index("lat"), 2)
    for row, edge_ref in ((1 - parity, near_ref), (parity, far_ref)):
        tap = 2 - 2 * row if transposed else 2 * row
        value = flat(edge_ref[...])
        parts = [product(value, weight_ref[3 * tap + lon_tap], transposed) for lon_tap in range(3)]
        total = total_ref[row] + aligned(*parts, lon_count, transposed)
        out_ref[:, row] = total.astype(out_ref.dtype).reshape(frames, lon_count, channels)


def start_of(offsets_ref, frame):
    total_frames = offsets_ref.shape[0]
    inside = jnp.clip(frame, 0, total_frames - 1)
    return jnp.clip(inside - offsets_ref[inside], 0, total_frames - 5)


def weight_of(offsets_ref, mixing_ref, frame, target):
    start = start_of(offsets_ref, frame)
    slot = target - start
    good = (slot >= 0) & (slot <= 4) & (frame >= 0) & (frame < offsets_ref.shape[0])
    weight = mixing_ref[pl.ds(jnp.where(good, 5 * (frame - start) + slot, 0), 1), :]
    return jnp.where(good, weight, 0.0)


LAGS = 2 * REACH + 1


def table_kernel(offsets_ref, mixing_ref, after_ref, reads_ref, read_by_ref):
    del after_ref
    frames = reads_ref.shape[0] // LAGS
    base = lax.axis_index("tm") * frames
    for frame in range(frames):
        for lag in range(-REACH, REACH + 1):
            row = frame * LAGS + lag + REACH
            here, there = base + frame, base + frame + lag
            reads_ref[row : row + 1, :] = weight_of(offsets_ref, mixing_ref, here, there)
            read_by_ref[row : row + 1, :] = weight_of(offsets_ref, mixing_ref, there, here)


def mixed(table_ref, sources, rows, total_of, store):
    frames = sources[0][0].shape[0]
    for frame in range(frames):
        for row in rows:
            total = total_of(frame, row)
            for ref, first in sources:
                for k in range(frames):
                    lag = first + k - frame
                    if abs(lag) <= REACH:
                        line = frame * LAGS + lag + REACH
                        term = table_ref[line : line + 1, :] * ref[k, row].astype(jnp.float32)
                        total = term if total is None else total + term
            store(frame, row, total)


def own_kernel(table_ref, own_ref, total_ref):
    def store(frame, row, total):
        total_ref[frame, row] = total

    mixed(table_ref, [(own_ref, 0)], range(2), lambda *_: None, store)


def sided(first_ref, second_ref, run):
    side = lax.rem(lax.axis_index("tm") + jnp.minimum(lax.axis_index("lat"), 1), 2)

    @pl.when(side == 1)
    def _():
        run(first_ref, second_ref)

    @pl.when(side == 0)
    def _():
        run(second_ref, first_ref)


def mid_kernel(table_ref, second_ref, total_ref, first_ref, hidden_ref, out_ref):
    frames = out_ref.shape[0]

    def store(frame, row, pre):
        sigma = 0.5 + 0.5 * jnp.tanh(0.5 * pre)
        slope = sigma * (1.0 + pre * (1.0 - sigma))
        out_ref[frame, row] = (hidden_ref[frame, row] * slope).astype(out_ref.dtype)

    def run(before, after):
        sources = [(before, -frames), (after, frames)]
        mixed(table_ref, sources, range(2), lambda frame, row: total_ref[frame, row], store)

    sided(first_ref, second_ref, run)


def hidden_kernel(cot_ref, proj_ref, out_ref):
    out_ref[...] = product(flat(cot_ref[...]), proj_ref[...], True).reshape(out_ref.shape)


def cut_kernel(x_ref, far_ref, near_ref):
    parity = lax.rem(lax.axis_index("lat"), 2)
    far_ref[...] = x_ref[:, parity]
    near_ref[...] = x_ref[:, 1 - parity]


def sum_kernel(far, table_ref, second_ref, total_ref, first_ref, out_ref):
    frames = out_ref.shape[0]
    parity = lax.rem(lax.axis_index("lat"), 2)
    row = parity if far else 1 - parity

    def store(frame, _, total):
        out_ref[frame] = total.astype(out_ref.dtype)

    def run(before, after):
        sources = [(before, -frames), (after, frames)]
        mixed(table_ref, sources, [row], lambda frame, _: total_ref[frame, row], store)

    sided(first_ref, second_ref, run)


def back_local_kernel(far_ref, near_ref, weight_ref, cot_ref, far_total, near_total):
    lon_count = far_ref.shape[1]
    parity = lax.rem(lax.axis_index("lat"), 2)
    far, near = flat(far_ref[...]), flat(near_ref[...])
    half = near.shape[0]
    both = jnp.concatenate([far, near], axis=0)
    tap = 2 * parity
    far_sums, near_sums = [], []
    for lon_tap in range(3):
        middle = product(both, weight_ref[3 + lon_tap], True)
        far_sums.append(middle[:half] + product(near, weight_ref[3 * tap + lon_tap], True))
        near_sums.append(middle[half:] + product(far, weight_ref[3 * (2 - tap) + lon_tap], True))
    for row, sums, out_ref in ((parity, far_sums, far_total), (1 - parity, near_sums, near_total)):
        out_ref[...] = aligned(*sums, lon_count, True) + flat(cot_ref[:, row]).astype(jnp.float32)


def back_halo(tap, total_ref, halo_ref, weight_ref, out_ref):
    value = flat(halo_ref[...])
    parts = [product(value, weight_ref[3 * tap + lon_tap], True) for lon_tap in range(3)]
    total = total_ref[...] + aligned(*parts, halo_ref.shape[1], True)
    out_ref[...] = total.astype(out_ref.dtype).reshape(out_ref.shape)


def final_kernel(far_total, far_halo, near_total, near_halo, weight_ref, out_ref, near_ref, far_ref, sems):
    parity = lax.rem(lax.axis_index("lat"), 2)
    back_halo(2 * parity, near_total, near_halo, weight_ref, near_ref)
    near_copy = pltpu.make_async_copy(near_ref, out_ref.at[:, 1 - parity], sems.at[0])
    near_copy.start()
    back_halo(2 - 2 * parity, far_total, far_halo, weight_ref, far_ref)
    far_copy = pltpu.make_async_copy(far_ref, out_ref.at[:, parity], sems.at[1])
    far_copy.start()
    near_copy.wait()
    far_copy.wait()


def call(kernel, out_shapes, specs, cost, out_specs=None, **extra):
    return pl.pallas_call(
        kernel,
        out_shape=out_shapes,
        in_specs=specs,
        out_specs=out_specs or jax.tree.map(lambda _: VMEM, out_shapes),
        compiler_params=pltpu.CompilerParams(vmem_limit_bytes=24 * 1024 * 1024),
        cost_estimate=pl.CostEstimate(flops=cost[0], bytes_accessed=cost[1], transcendentals=0),
        **extra,
    )


def convolve(block, far, near, weight, transposed, *added):
    frames, row_count, lon_count, channels = block.shape
    half = 2 * 3 * frames * row_count * lon_count * channels * channels
    sums = jax.ShapeDtypeStruct((row_count, frames * lon_count, channels), jnp.float32)
    total = call(
        functools.partial(local_kernel, transposed), sums, [VMEM] * (2 + len(added)), (2 * half, 2_000_000)
    )(block, weight, *added)
    far, near = swap(far, "lat", 1), swap(near, "lat", 0)
    result = jax.ShapeDtypeStruct(block.shape, jnp.bfloat16)
    return call(functools.partial(halo_kernel, transposed), result, [VMEM] * 4, (half, 2_000_000))(
        total, far, near, weight
    )


def body(trajectory, cotangent, conv_weight, proj_weight, mixing, offsets):
    frames, row_count, lon_count, channels = trajectory.shape
    block = jax.ShapeDtypeStruct(trajectory.shape, jnp.bfloat16)
    edge = jax.ShapeDtypeStruct((frames, lon_count, channels), jnp.bfloat16)
    far, near = call(cut_kernel, (edge, edge), [VMEM], (4_000_000_000, 600_000))(trajectory)
    wide = jax.ShapeDtypeStruct(trajectory.shape, jnp.float32)
    conv_out = convolve(trajectory, far, near, conv_weight, False)
    table = jax.ShapeDtypeStruct((frames * LAGS, channels), jnp.float32)
    reads, read_by = call(table_kernel, (table, table), [SMEM] + [VMEM] * 2, (1_000_000, 200_000))(
        offsets, mixing, conv_out
    )
    first, second = crossed(conv_out, 0), crossed(conv_out, 1)
    hidden = call(hidden_kernel, wide, [VMEM] * 2, (67_000_000, 1_000_000))(cotangent, proj_weight)
    own = call(own_kernel, wide, [VMEM] * 2, (10_000_000, 1_000_000))(reads, conv_out)
    g_pre = call(mid_kernel, block, [VMEM] * 5, (10_000_000, 1_400_000))(reads, second, own, first, hidden)
    first, second = crossed(g_pre, 0), crossed(g_pre, 1)
    own = call(own_kernel, wide, [VMEM] * 2, (10_000_000, 1_000_000))(read_by, g_pre)
    far, near = [
        call(functools.partial(sum_kernel, is_far), edge, [VMEM] * 4, (5_000_000, 700_000))(
            read_by, second, own, first
        )
        for is_far in (True, False)
    ]
    far_halo, near_halo = swap(far, "lat", 1), swap(near, "lat", 0)
    tap = 2 * 3 * frames * lon_count * channels * channels
    sums = jax.ShapeDtypeStruct((frames * lon_count, channels), jnp.float32)
    far_total, near_total = call(back_local_kernel, (sums, sums), [VMEM] * 4, (4 * tap, 2_000_000))(
        far, near, conv_weight, cotangent
    )
    return call(
        final_kernel, block, [VMEM] * 5, (2 * tap, 2_000_000), out_specs=pl.BlockSpec(memory_space=pl.ANY),
        scratch_shapes=[pltpu.VMEM(edge.shape, edge.dtype)] * 2 + [pltpu.SemaphoreType.DMA((2,))],
    )(far_total, far_halo, near_total, near_halo, conv_weight)


def solution(mesh):
    in_specs = (P("tm", "lat", None, None), P("tm", "lat", None, None), P(), P(), P(), P())
    out_specs = P("tm", "lat", None, None)
    return jax.shard_map(body, mesh=mesh, in_specs=in_specs, out_specs=out_specs, check_vma=False)
```

```python
import functools

import jax
import jax.numpy as jnp
import numpy as np
from jax import lax
from jax.experimental import pallas as pl
from jax.experimental.pallas import tpu as pltpu
from jax.sharding import PartitionSpec as P

VMEM = pl.BlockSpec(memory_space=pltpu.VMEM)
SMEM = pl.BlockSpec(memory_space=pltpu.SMEM)
REACH = 4


def swap(value, axis, offset):
    size = lax.axis_size(axis)
    pairs = [(i, i + 1) for i in range(offset, size - 1, 2)]
    return lax.ppermute(value, axis, pairs + [(j, i) for i, j in pairs])


def turn_of(link, band, where):
    place = link % 16
    plain = 2 * (place % 2)
    turned = where(place % 8 == 7, 1, where(place < 8, plain, 2 - plain))
    return where(band == 0, plain, turned)


def crossed(value, turn):
    frames, bands = lax.axis_size("tm"), lax.axis_size("lat")
    pairs = [
        (i * bands + band, (i + 1) * bands + band)
        for band in range(bands)
        for i in range(frames - 1)
        if turn_of(i, band, np.where) == turn
    ]
    return lax.ppermute(value, ("tm", "lat"), pairs + [(j, i) for i, j in pairs])


def product(value, matrix, transposed):
    return lax.dot_general(
        value,
        matrix,
        (((1,), (1 if transposed else 0,)), ((), ())),
        preferred_element_type=jnp.float32,
    )


def rolled(value, lon_count, step):
    split = value.reshape(-1, lon_count, value.shape[-1])
    return pltpu.roll(split, step % lon_count, axis=1).reshape(value.shape)


def aligned(low, mid, high, lon_count, transposed):
    step = -1 if transposed else 1
    return mid + rolled(low, lon_count, step) + rolled(high, lon_count, -step)


def flat(value):
    return value.reshape(-1, value.shape[-1])


def local_kernel(transposed, x_ref, weight_ref, *refs):
    total_ref = refs[-1]
    lon_count = x_ref.shape[2]
    first, second = flat(x_ref[:, 0]), flat(x_ref[:, 1])
    half = first.shape[0]
    both = jnp.concatenate([first, second], axis=0)
    ahead, behind = (0, 2) if transposed else (2, 0)
    sums = [[], []]
    for lon_tap in range(3):
        middle = product(both, weight_ref[3 + lon_tap], transposed)
        sums[0].append(middle[:half] + product(second, weight_ref[3 * ahead + lon_tap], transposed))
        sums[1].append(middle[half:] + product(first, weight_ref[3 * behind + lon_tap], transposed))
    for row in range(2):
        total_ref[row] = aligned(*sums[row], lon_count, transposed)


def halo_kernel(transposed, total_ref, far_ref, near_ref, weight_ref, out_ref):
    frames, lon_count, channels = far_ref.shape
    parity = lax.rem(lax.axis_index("lat"), 2)
    for row, edge_ref in ((1 - parity, near_ref), (parity, far_ref)):
        tap = 2 - 2 * row if transposed else 2 * row
        value = flat(edge_ref[...])
        parts = [product(value, weight_ref[3 * tap + lon_tap], transposed) for lon_tap in range(3)]
        total = total_ref[row] + aligned(*parts, lon_count, transposed)
        out_ref[:, row] = total.astype(out_ref.dtype).reshape(frames, lon_count, channels)


def start_of(offsets_ref, frame):
    total_frames = offsets_ref.shape[0]
    inside = jnp.clip(frame, 0, total_frames - 1)
    return jnp.clip(inside - offsets_ref[inside], 0, total_frames - 5)


def weight_of(offsets_ref, mixing_ref, frame, target):
    start = start_of(offsets_ref, frame)
    slot = target - start
    good = (slot >= 0) & (slot <= 4) & (frame >= 0) & (frame < offsets_ref.shape[0])
    weight = mixing_ref[pl.ds(jnp.where(good, 5 * (frame - start) + slot, 0), 1), :]
    return jnp.where(good, weight, 0.0)


LAGS = 2 * REACH + 1


def table_kernel(offsets_ref, mixing_ref, after_ref, reads_ref, read_by_ref):
    del after_ref
    frames = reads_ref.shape[0] // LAGS
    base = lax.axis_index("tm") * frames
    for frame in range(frames):
        for lag in range(-REACH, REACH + 1):
            row = frame * LAGS + lag + REACH
            here, there = base + frame, base + frame + lag
            reads_ref[row : row + 1, :] = weight_of(offsets_ref, mixing_ref, here, there)
            read_by_ref[row : row + 1, :] = weight_of(offsets_ref, mixing_ref, there, here)


def mixed(table_ref, sources, rows, total_of, store):
    frames = sources[0][0].shape[0]
    for frame in range(frames):
        for row in rows:
            total = total_of(frame, row)
            for ref, first in sources:
                for k in range(frames):
                    lag = first + k - frame
                    if abs(lag) <= REACH:
                        line = frame * LAGS + lag + REACH
                        term = table_ref[line : line + 1, :] * ref[k, row].astype(jnp.float32)
                        total = term if total is None else total + term
            store(frame, row, total)


def own_kernel(table_ref, own_ref, total_ref):
    def store(frame, row, total):
        total_ref[frame, row] = total

    mixed(table_ref, [(own_ref, 0)], range(2), lambda *_: None, store)


def sided(refs, run):
    block, band = lax.axis_index("tm"), lax.axis_index("lat")
    left, right = turn_of(block + 15, band, jnp.where), turn_of(block, band, jnp.where)
    for i in range(3):
        for j in range(3):
            if i != j:
                pl.when((left == i) & (right == j))(functools.partial(run, refs[i], refs[j]))


def mid_kernel(table_ref, third_ref, second_ref, first_ref, total_ref, hidden_ref, out_ref):
    frames = out_ref.shape[0]

    def store(frame, row, pre):
        sigma = 0.5 + 0.5 * jnp.tanh(0.5 * pre)
        slope = sigma * (1.0 + pre * (1.0 - sigma))
        out_ref[frame, row] = (hidden_ref[frame, row] * slope).astype(out_ref.dtype)

    def run(before, after):
        sources = [(before, -frames), (after, frames)]
        mixed(table_ref, sources, range(2), lambda frame, row: total_ref[frame, row], store)

    sided((first_ref, second_ref, third_ref), run)


def hidden_kernel(cot_ref, proj_ref, out_ref):
    out_ref[...] = product(flat(cot_ref[...]), proj_ref[...], True).reshape(out_ref.shape)


def cut_kernel(x_ref, far_ref, near_ref):
    parity = lax.rem(lax.axis_index("lat"), 2)
    far_ref[...] = x_ref[:, parity]
    near_ref[...] = x_ref[:, 1 - parity]


def sum_kernel(far, table_ref, third_ref, second_ref, first_ref, total_ref, out_ref):
    frames = out_ref.shape[0]
    parity = lax.rem(lax.axis_index("lat"), 2)
    row = parity if far else 1 - parity

    def store(frame, _, total):
        out_ref[frame] = total.astype(out_ref.dtype)

    def run(before, after):
        sources = [(before, -frames), (after, frames)]
        mixed(table_ref, sources, [row], lambda frame, _: total_ref[frame, row], store)

    sided((first_ref, second_ref, third_ref), run)


def back_local_kernel(far_ref, near_ref, weight_ref, cot_ref, far_total, near_total):
    lon_count = far_ref.shape[1]
    parity = lax.rem(lax.axis_index("lat"), 2)
    far, near = flat(far_ref[...]), flat(near_ref[...])
    half = near.shape[0]
    both = jnp.concatenate([far, near], axis=0)
    tap = 2 * parity
    far_sums, near_sums = [], []
    for lon_tap in range(3):
        middle = product(both, weight_ref[3 + lon_tap], True)
        far_sums.append(middle[:half] + product(near, weight_ref[3 * tap + lon_tap], True))
        near_sums.append(middle[half:] + product(far, weight_ref[3 * (2 - tap) + lon_tap], True))
    for row, sums, out_ref in ((parity, far_sums, far_total), (1 - parity, near_sums, near_total)):
        out_ref[...] = aligned(*sums, lon_count, True) + flat(cot_ref[:, row]).astype(jnp.float32)


def back_halo(tap, total_ref, halo_ref, weight_ref, out_ref):
    value = flat(halo_ref[...])
    parts = [product(value, weight_ref[3 * tap + lon_tap], True) for lon_tap in range(3)]
    total = total_ref[...] + aligned(*parts, halo_ref.shape[1], True)
    out_ref[...] = total.astype(out_ref.dtype).reshape(out_ref.shape)


def final_kernel(far_total, far_halo, near_total, near_halo, weight_ref, out_ref, near_ref, far_ref, sems):
    parity = lax.rem(lax.axis_index("lat"), 2)
    back_halo(2 * parity, near_total, near_halo, weight_ref, near_ref)
    near_copy = pltpu.make_async_copy(near_ref, out_ref.at[:, 1 - parity], sems.at[0])
    near_copy.start()
    back_halo(2 - 2 * parity, far_total, far_halo, weight_ref, far_ref)
    far_copy = pltpu.make_async_copy(far_ref, out_ref.at[:, parity], sems.at[1])
    far_copy.start()
    near_copy.wait()
    far_copy.wait()


def call(kernel, out_shapes, specs, cost, out_specs=None, **extra):
    return pl.pallas_call(
        kernel,
        out_shape=out_shapes,
        in_specs=specs,
        out_specs=out_specs or jax.tree.map(lambda _: VMEM, out_shapes),
        compiler_params=pltpu.CompilerParams(vmem_limit_bytes=24 * 1024 * 1024),
        cost_estimate=pl.CostEstimate(flops=cost[0], bytes_accessed=cost[1], transcendentals=0),
        **extra,
    )


def convolve(block, far, near, weight, transposed, *added):
    frames, row_count, lon_count, channels = block.shape
    half = 2 * 3 * frames * row_count * lon_count * channels * channels
    sums = jax.ShapeDtypeStruct((row_count, frames * lon_count, channels), jnp.float32)
    total = call(
        functools.partial(local_kernel, transposed), sums, [VMEM] * (2 + len(added)), (2 * half, 2_000_000)
    )(block, weight, *added)
    far, near = swap(far, "lat", 1), swap(near, "lat", 0)
    result = jax.ShapeDtypeStruct(block.shape, jnp.bfloat16)
    return call(functools.partial(halo_kernel, transposed), result, [VMEM] * 4, (half, 2_000_000))(
        total, far, near, weight
    )


def body(trajectory, cotangent, conv_weight, proj_weight, mixing, offsets):
    frames, row_count, lon_count, channels = trajectory.shape
    block = jax.ShapeDtypeStruct(trajectory.shape, jnp.bfloat16)
    edge = jax.ShapeDtypeStruct((frames, lon_count, channels), jnp.bfloat16)
    far, near = call(cut_kernel, (edge, edge), [VMEM], (4_000_000_000, 600_000))(trajectory)
    wide = jax.ShapeDtypeStruct(trajectory.shape, jnp.float32)
    conv_out = convolve(trajectory, far, near, conv_weight, False)
    table = jax.ShapeDtypeStruct((frames * LAGS, channels), jnp.float32)
    reads, read_by = call(table_kernel, (table, table), [SMEM] + [VMEM] * 2, (1_000_000, 200_000))(
        offsets, mixing, conv_out
    )
    first, second, third = [crossed(conv_out, turn) for turn in range(3)]
    hidden = call(hidden_kernel, wide, [VMEM] * 2, (67_000_000, 1_000_000))(cotangent, proj_weight)
    own = call(own_kernel, wide, [VMEM] * 2, (10_000_000, 1_000_000))(reads, conv_out)
    g_pre = call(mid_kernel, block, [VMEM] * 6, (10_000_000, 1_400_000))(
        reads, third, second, first, own, hidden
    )
    first, second, third = [crossed(g_pre, turn) for turn in range(3)]
    own = call(own_kernel, wide, [VMEM] * 2, (10_000_000, 1_000_000))(read_by, g_pre)
    far, near = [
        call(functools.partial(sum_kernel, is_far), edge, [VMEM] * 5, (5_000_000, 700_000))(
            read_by, third, second, first, own
        )
        for is_far in (True, False)
    ]
    far_halo, near_halo = swap(far, "lat", 1), swap(near, "lat", 0)
    tap = 2 * 3 * frames * lon_count * channels * channels
    sums = jax.ShapeDtypeStruct((frames * lon_count, channels), jnp.float32)
    far_total, near_total = call(back_local_kernel, (sums, sums), [VMEM] * 4, (4 * tap, 2_000_000))(
        far, near, conv_weight, cotangent
    )
    return call(
        final_kernel, block, [VMEM] * 5, (2 * tap, 2_000_000), out_specs=pl.BlockSpec(memory_space=pl.ANY),
        scratch_shapes=[pltpu.VMEM(edge.shape, edge.dtype)] * 2 + [pltpu.SemaphoreType.DMA((2,))],
    )(far_total, far_halo, near_total, near_halo, conv_weight)


def solution(mesh):
    in_specs = (P("tm", "lat", None, None), P("tm", "lat", None, None), P(), P(), P(), P())
    out_specs = P("tm", "lat", None, None)
    return jax.shard_map(body, mesh=mesh, in_specs=in_specs, out_specs=out_specs, check_vma=False)
```

```python
import functools

import jax
import jax.numpy as jnp
import numpy as np
from jax import lax
from jax.experimental import pallas as pl
from jax.experimental.pallas import tpu as pltpu
from jax.sharding import PartitionSpec as P

VMEM = pl.BlockSpec(memory_space=pltpu.VMEM)
SMEM = pl.BlockSpec(memory_space=pltpu.SMEM)
REACH = 4


def swap(value, axis, offset):
    size = lax.axis_size(axis)
    pairs = [(i, i + 1) for i in range(offset, size - 1, 2)]
    return lax.ppermute(value, axis, pairs + [(j, i) for i, j in pairs])


def turn_of(link, band, where):
    place = link % 16
    plain = 2 * (place % 2)
    turned = where(place % 8 == 7, 1, where(place < 8, plain, 2 - plain))
    return where(band == 0, place % 2, turned)


def crossed(value, turn):
    frames, bands = lax.axis_size("tm"), lax.axis_size("lat")
    pairs = [
        (i * bands + band, (i + 1) * bands + band)
        for band in range(bands)
        for i in range(frames - 1)
        if turn_of(i, band, np.where) == turn
    ]
    return lax.ppermute(value, ("tm", "lat"), pairs + [(j, i) for i, j in pairs])


def product(value, matrix, transposed):
    return lax.dot_general(
        value,
        matrix,
        (((1,), (1 if transposed else 0,)), ((), ())),
        preferred_element_type=jnp.float32,
    )


def rolled(value, lon_count, step):
    split = value.reshape(-1, lon_count, value.shape[-1])
    return pltpu.roll(split, step % lon_count, axis=1).reshape(value.shape)


def aligned(low, mid, high, lon_count, transposed):
    step = -1 if transposed else 1
    return mid + rolled(low, lon_count, step) + rolled(high, lon_count, -step)


def flat(value):
    return value.reshape(-1, value.shape[-1])


def local_kernel(transposed, x_ref, weight_ref, *refs):
    total_ref = refs[-1]
    lon_count = x_ref.shape[2]
    first, second = flat(x_ref[:, 0]), flat(x_ref[:, 1])
    half = first.shape[0]
    both = jnp.concatenate([first, second], axis=0)
    ahead, behind = (0, 2) if transposed else (2, 0)
    sums = [[], []]
    for lon_tap in range(3):
        middle = product(both, weight_ref[3 + lon_tap], transposed)
        sums[0].append(middle[:half] + product(second, weight_ref[3 * ahead + lon_tap], transposed))
        sums[1].append(middle[half:] + product(first, weight_ref[3 * behind + lon_tap], transposed))
    for row in range(2):
        total_ref[row] = aligned(*sums[row], lon_count, transposed)


def halo_kernel(transposed, total_ref, far_ref, near_ref, weight_ref, out_ref):
    frames, lon_count, channels = far_ref.shape
    parity = lax.rem(lax.axis_index("lat"), 2)
    for row, edge_ref in ((1 - parity, near_ref), (parity, far_ref)):
        tap = 2 - 2 * row if transposed else 2 * row
        value = flat(edge_ref[...])
        parts = [product(value, weight_ref[3 * tap + lon_tap], transposed) for lon_tap in range(3)]
        total = total_ref[row] + aligned(*parts, lon_count, transposed)
        out_ref[:, row] = total.astype(out_ref.dtype).reshape(frames, lon_count, channels)


def start_of(offsets_ref, frame):
    total_frames = offsets_ref.shape[0]
    inside = jnp.clip(frame, 0, total_frames - 1)
    return jnp.clip(inside - offsets_ref[inside], 0, total_frames - 5)


def weight_of(offsets_ref, mixing_ref, frame, target):
    start = start_of(offsets_ref, frame)
    slot = target - start
    good = (slot >= 0) & (slot <= 4) & (frame >= 0) & (frame < offsets_ref.shape[0])
    weight = mixing_ref[pl.ds(jnp.where(good, 5 * (frame - start) + slot, 0), 1), :]
    return jnp.where(good, weight, 0.0)


LAGS = 2 * REACH + 1


def table_kernel(offsets_ref, mixing_ref, after_ref, reads_ref, read_by_ref):
    del after_ref
    frames = reads_ref.shape[0] // LAGS
    base = lax.axis_index("tm") * frames
    for frame in range(frames):
        for lag in range(-REACH, REACH + 1):
            row = frame * LAGS + lag + REACH
            here, there = base + frame, base + frame + lag
            reads_ref[row : row + 1, :] = weight_of(offsets_ref, mixing_ref, here, there)
            read_by_ref[row : row + 1, :] = weight_of(offsets_ref, mixing_ref, there, here)


def mixed(table_ref, sources, rows, total_of, store):
    frames = sources[0][0].shape[0]
    for frame in range(frames):
        for row in rows:
            total = total_of(frame, row)
            for ref, first in sources:
                for k in range(frames):
                    lag = first + k - frame
                    if abs(lag) <= REACH:
                        line = frame * LAGS + lag + REACH
                        term = table_ref[line : line + 1, :] * ref[k, row].astype(jnp.float32)
                        total = term if total is None else total + term
            store(frame, row, total)


def own_kernel(table_ref, own_ref, total_ref):
    def store(frame, row, total):
        total_ref[frame, row] = total

    mixed(table_ref, [(own_ref, 0)], range(2), lambda *_: None, store)


def sided(refs, run):
    block, band = lax.axis_index("tm"), lax.axis_index("lat")
    left, right = turn_of(block + 15, band, jnp.where), turn_of(block, band, jnp.where)
    for i in range(3):
        for j in range(3):
            if i != j:
                pl.when((left == i) & (right == j))(functools.partial(run, refs[i], refs[j]))


def mid_kernel(table_ref, third_ref, second_ref, first_ref, total_ref, hidden_ref, out_ref):
    frames = out_ref.shape[0]

    def store(frame, row, pre):
        sigma = 0.5 + 0.5 * jnp.tanh(0.5 * pre)
        slope = sigma * (1.0 + pre * (1.0 - sigma))
        out_ref[frame, row] = (hidden_ref[frame, row] * slope).astype(out_ref.dtype)

    def run(before, after):
        sources = [(before, -frames), (after, frames)]
        mixed(table_ref, sources, range(2), lambda frame, row: total_ref[frame, row], store)

    sided((first_ref, second_ref, third_ref), run)


def hidden_kernel(cot_ref, proj_ref, out_ref):
    out_ref[...] = product(flat(cot_ref[...]), proj_ref[...], True).reshape(out_ref.shape)


def cut_kernel(x_ref, far_ref, near_ref):
    parity = lax.rem(lax.axis_index("lat"), 2)
    far_ref[...] = x_ref[:, parity]
    near_ref[...] = x_ref[:, 1 - parity]


def sum_kernel(far, table_ref, third_ref, second_ref, first_ref, total_ref, out_ref):
    frames = out_ref.shape[0]
    parity = lax.rem(lax.axis_index("lat"), 2)
    row = parity if far else 1 - parity

    def store(frame, _, total):
        out_ref[frame] = total.astype(out_ref.dtype)

    def run(before, after):
        sources = [(before, -frames), (after, frames)]
        mixed(table_ref, sources, [row], lambda frame, _: total_ref[frame, row], store)

    sided((first_ref, second_ref, third_ref), run)


def back_local_kernel(far_ref, near_ref, weight_ref, cot_ref, far_total, near_total):
    lon_count = far_ref.shape[1]
    parity = lax.rem(lax.axis_index("lat"), 2)
    far, near = flat(far_ref[...]), flat(near_ref[...])
    half = near.shape[0]
    both = jnp.concatenate([far, near], axis=0)
    tap = 2 * parity
    far_sums, near_sums = [], []
    for lon_tap in range(3):
        middle = product(both, weight_ref[3 + lon_tap], True)
        far_sums.append(middle[:half] + product(near, weight_ref[3 * tap + lon_tap], True))
        near_sums.append(middle[half:] + product(far, weight_ref[3 * (2 - tap) + lon_tap], True))
    for row, sums, out_ref in ((parity, far_sums, far_total), (1 - parity, near_sums, near_total)):
        out_ref[...] = aligned(*sums, lon_count, True) + flat(cot_ref[:, row]).astype(jnp.float32)


def back_halo(tap, total_ref, halo_ref, weight_ref, out_ref):
    value = flat(halo_ref[...])
    parts = [product(value, weight_ref[3 * tap + lon_tap], True) for lon_tap in range(3)]
    total = total_ref[...] + aligned(*parts, halo_ref.shape[1], True)
    out_ref[...] = total.astype(out_ref.dtype).reshape(out_ref.shape)


def final_kernel(far_total, far_halo, near_total, near_halo, weight_ref, out_ref, near_ref, far_ref, sems):
    parity = lax.rem(lax.axis_index("lat"), 2)
    back_halo(2 * parity, near_total, near_halo, weight_ref, near_ref)
    near_copy = pltpu.make_async_copy(near_ref, out_ref.at[:, 1 - parity], sems.at[0])
    near_copy.start()
    back_halo(2 - 2 * parity, far_total, far_halo, weight_ref, far_ref)
    far_copy = pltpu.make_async_copy(far_ref, out_ref.at[:, parity], sems.at[1])
    far_copy.start()
    near_copy.wait()
    far_copy.wait()


def call(kernel, out_shapes, specs, cost, out_specs=None, **extra):
    return pl.pallas_call(
        kernel,
        out_shape=out_shapes,
        in_specs=specs,
        out_specs=out_specs or jax.tree.map(lambda _: VMEM, out_shapes),
        compiler_params=pltpu.CompilerParams(vmem_limit_bytes=24 * 1024 * 1024),
        cost_estimate=pl.CostEstimate(flops=cost[0], bytes_accessed=cost[1], transcendentals=0),
        **extra,
    )


def convolve(block, far, near, weight, transposed, *added):
    frames, row_count, lon_count, channels = block.shape
    half = 2 * 3 * frames * row_count * lon_count * channels * channels
    sums = jax.ShapeDtypeStruct((row_count, frames * lon_count, channels), jnp.float32)
    total = call(
        functools.partial(local_kernel, transposed), sums, [VMEM] * (2 + len(added)), (2 * half, 2_000_000)
    )(block, weight, *added)
    far, near = swap(far, "lat", 1), swap(near, "lat", 0)
    result = jax.ShapeDtypeStruct(block.shape, jnp.bfloat16)
    return call(functools.partial(halo_kernel, transposed), result, [VMEM] * 4, (half, 2_000_000))(
        total, far, near, weight
    )


def body(trajectory, cotangent, conv_weight, proj_weight, mixing, offsets):
    frames, row_count, lon_count, channels = trajectory.shape
    block = jax.ShapeDtypeStruct(trajectory.shape, jnp.bfloat16)
    edge = jax.ShapeDtypeStruct((frames, lon_count, channels), jnp.bfloat16)
    far, near = call(cut_kernel, (edge, edge), [VMEM], (4_000_000_000, 600_000))(trajectory)
    wide = jax.ShapeDtypeStruct(trajectory.shape, jnp.float32)
    conv_out = convolve(trajectory, far, near, conv_weight, False)
    table = jax.ShapeDtypeStruct((frames * LAGS, channels), jnp.float32)
    reads, read_by = call(table_kernel, (table, table), [SMEM] + [VMEM] * 2, (1_000_000, 200_000))(
        offsets, mixing, conv_out
    )
    first, second, third = [crossed(conv_out, turn) for turn in range(3)]
    hidden = call(hidden_kernel, wide, [VMEM] * 2, (67_000_000, 1_000_000))(cotangent, proj_weight)
    own = call(own_kernel, wide, [VMEM] * 2, (10_000_000, 1_000_000))(reads, conv_out)
    g_pre = call(mid_kernel, block, [VMEM] * 6, (10_000_000, 1_400_000))(
        reads, third, second, first, own, hidden
    )
    first, second, third = [crossed(g_pre, turn) for turn in range(3)]
    own = call(own_kernel, wide, [VMEM] * 2, (10_000_000, 1_000_000))(read_by, g_pre)
    far, near = [
        call(functools.partial(sum_kernel, is_far), edge, [VMEM] * 5, (5_000_000, 700_000))(
            read_by, third, second, first, own
        )
        for is_far in (True, False)
    ]
    far_halo, near_halo = swap(far, "lat", 1), swap(near, "lat", 0)
    tap = 2 * 3 * frames * lon_count * channels * channels
    sums = jax.ShapeDtypeStruct((frames * lon_count, channels), jnp.float32)
    far_total, near_total = call(back_local_kernel, (sums, sums), [VMEM] * 4, (4 * tap, 2_000_000))(
        far, near, conv_weight, cotangent
    )
    return call(
        final_kernel, block, [VMEM] * 5, (2 * tap, 2_000_000), out_specs=pl.BlockSpec(memory_space=pl.ANY),
        scratch_shapes=[pltpu.VMEM(edge.shape, edge.dtype)] * 2 + [pltpu.SemaphoreType.DMA((2,))],
    )(far_total, far_halo, near_total, near_halo, conv_weight)


def solution(mesh):
    in_specs = (P("tm", "lat", None, None), P("tm", "lat", None, None), P(), P(), P(), P())
    out_specs = P("tm", "lat", None, None)
    return jax.shard_map(body, mesh=mesh, in_specs=in_specs, out_specs=out_specs, check_vma=False)
```
